32 devices in a mesh: prow: 4 (over z), pcol: 8 (over y, x, core).
Axes of the slice: x: 2, y: 2, z: 4, core: 2. Of those that a mesh axis runs over, the one named last changes fastest.
Arguments:
- right_sides: bfloat16 [8, 1, 8, 4, 128, 128], P(None, None, 'pcol', 'prow'), may hold values from -6 to 6
- inverses: bfloat16 [8, 1, 8, 4, 128, 128], P(None, None, 'pcol', 'prow'), as said below
- blocks: bfloat16 [7, 1, 8, 4, 4, 8, 128, 128], P(None, None, 'pcol', None, 'prow'), may hold values from -0.0546875 to 0.0546875
- targets: int32 [7, 1, 8, 4, 4, 8], P(None, None, 'pcol', None, 'prow'), may hold values from 32 to 255, as said below
Outputs:
- solution: bfloat16 [8, 1, 8, 4, 128, 128], P(None, None, 'pcol', 'prow')
The draws below stay inside these ranges and needn't reach their ends.
Inputs may be any that keep to these rules, and one draw needn't show every extreme that they name: `targets`: entry [l, g, c, s, r, m] is the number of a supernode on a level above l whose number is congruent to r modulo 4; numbers may repeat. `inverses`: each block is well conditioned, with a diagonal near one.
All inputs are finite; a program needn't handle non-finite values.
Results may differ from the reference program's by a relative error of at most 0.007.
Values may be sent and summed in bfloat16 or wider, within the bound.
A program may use at most 128 MiB of HBM per device.

```python
import math
import jax
import jax.numpy as jnp
from jax import lax

S = 128
R = 128
LEV = 8
NBR = 8
G = 1
PROWS = 4
PCOLS = 8


def draw_inverses(key, part):
    full_shape = (LEV, G, PCOLS, PROWS, S, S)
    noise_part = jax.random.normal(key, full_shape, jnp.float32)
    diag_gain = jax.random.uniform(jax.random.fold_in(key, 7), full_shape[:-1], jnp.float32, 0.7, 1.3)
    identity = jnp.eye(S, dtype=jnp.float32)
    return (identity * diag_gain[..., None] + 0.25 / math.sqrt(S) * noise_part).astype(jnp.bfloat16)


def draw_targets(key, part):
    full_shape = (LEV - 1, G, PCOLS, PROWS, PROWS, NBR)
    tier_iota = lax.broadcasted_iota(jnp.int32, full_shape, 0)
    row_iota = lax.broadcasted_iota(jnp.int32, full_shape, 4)
    span_left = LEV - 1 - tier_iota
    raw_bits = jax.random.randint(jax.random.fold_in(key, 1), full_shape, 0, 1 << 20)
    higher = tier_iota + 1 + raw_bits % span_left
    group_pick = jax.random.randint(jax.random.fold_in(key, 2), full_shape, 0, G)
    column_pick = jax.random.randint(jax.random.fold_in(key, 3), full_shape, 0, PCOLS)
    per_tier = G * PROWS * PCOLS
    numbers = higher * per_tier + (group_pick * PCOLS + column_pick) * PROWS + row_iota
    total_count = (LEV - 1) * G * PCOLS * PROWS * PROWS * NBR
    flat_index = jnp.arange(total_count, dtype=jnp.int32).reshape(full_shape)
    numbers = jnp.where(flat_index == 0, per_tier, numbers)
    numbers = jnp.where(flat_index == total_count - 1, LEV * per_tier - 1, numbers)
    return numbers.astype(jnp.int32)


def steps_of(own_key, extent, split, least, largest):
    def one(position, shards_of):
        steps = jax.random.uniform(jax.random.fold_in(jax.random.fold_in(own_key, 6), position), (shards_of,), jnp.float32, least / len(split), largest / len(split))
        return jnp.repeat(jnp.exp(steps), extent[position] // shards_of).reshape((-1,) + (1,) * (len(extent) - position - 1))

    gain = one(*split[0])
    for cut in split[1:]:
        gain = gain * one(*cut)
    return gain


def normal_values(own_key, dims, spread, reach, cuts=(), kind=jnp.bfloat16):
    values = spread * jax.random.normal(own_key, dims, jnp.float32)
    if cuts:
        values = values * steps_of(own_key, dims, cuts, -0.22, 0.18)
    return jnp.clip(values, -reach, reach).astype(kind)


def setup_inputs(seed: int = 0) -> dict:
    splits = jax.random.split(jax.random.key(seed), 5)
    return {
        "right_sides": normal_values(splits[0], (LEV, G, PCOLS, PROWS, S, R), 1.0, 6.0, ((2, 8), (3, 4))),
        "inverses": draw_inverses(jax.random.fold_in(splits[4], 71), 0),
        "blocks": normal_values(splits[2], (LEV - 1, G, PCOLS, PROWS, PROWS, NBR, S, S), (3 * S * NBR * PROWS) ** -0.5, 0.0546875, ((2, 8), (4, 4))),
        "targets": draw_targets(jax.random.fold_in(splits[4], 71), 0),
    }


def reference(right_sides, inverses, blocks, targets):
    per_tier = G * PROWS * PCOLS
    pending = jnp.zeros((LEV * per_tier, S, R), jnp.float32)
    solved_tiers = []
    for tier_index in range(LEV):
        incoming = pending[tier_index * per_tier:(tier_index + 1) * per_tier]
        residual = (right_sides[tier_index].reshape(per_tier, S, R).astype(jnp.float32) - incoming).astype(jnp.bfloat16)
        inverse_tier = inverses[tier_index].reshape(per_tier, S, S)
        solution = jnp.einsum("nij,njk->nik", inverse_tier.astype(jnp.float32), residual.astype(jnp.float32)).astype(jnp.bfloat16)
        solved_tiers.append(solution)
        if tier_index + 1 < LEV:
            sources = solution.reshape(G, PCOLS, PROWS, S, R).astype(jnp.float32)
            products = jnp.einsum("gcsrmij,gcsjk->gcsrmik", blocks[tier_index].astype(jnp.float32), sources)
            pending = pending.at[targets[tier_index].reshape(-1)].add(products.reshape(-1, S, R))
    return jnp.stack(solved_tiers).reshape(LEV, G, PCOLS, PROWS, S, R)
```

```python
import functools

import jax
import jax.numpy as jnp
from jax import lax
from jax.experimental import pallas as pl
from jax.experimental.pallas import tpu as pltpu
from jax.sharding import PartitionSpec as P

MESH = pl.DeviceIdType.MESH
CHUNKS = 2
GROUP = 4
F32 = jnp.float32
BF16 = jnp.bfloat16


def dot_nt(a, b):
    return lax.dot_general(a, b, (((1,), (1,)), ((), ())), preferred_element_type=F32)


def flip(a, k, n):
    total = 0
    w = 1
    while w < n:
        total = total + lax.rem(a // w + k // w, 2) * w
        w *= 2
    return total


def kernel(
    dims,
    table,
    slots,
    rs,
    inv,
    blocks,
    out,
    raw,
    merged,
    xs,
    part_in,
    part_out,
    acc,
    own,
    rst,
    load_sem,
    xsend,
    xrecv,
    psend,
    precv,
):
    levels, rows, cols, nbr, size, rhs = dims
    steps = levels - 1
    per = rows * nbr
    half = rhs // CHUNKS
    r = lax.axis_index("prow")
    c = lax.axis_index("pcol")

    col_order = sorted(range(1, cols), key=lambda k: (-bin(k // 2).count("1"), k % 2, k))
    row_order = list(range(rows - 1, 0, -1))
    col_peer = [flip(c, k, cols) for k in range(cols)]
    row_peer = [flip(r, k, rows) for k in range(rows)]

    def load(l):
        return pltpu.make_async_copy(blocks.at[l], raw.at[l], load_sem.at[l])

    for l in range(steps):
        load(l).start()

    barrier = pltpu.get_barrier_semaphore()
    for k in range(1, cols):
        pl.semaphore_signal(
            barrier, inc=1, device_id={"pcol": col_peer[k]}, device_id_type=MESH
        )
    for k in range(1, rows):
        pl.semaphore_signal(
            barrier, inc=1, device_id={"prow": row_peer[k]}, device_id_type=MESH
        )

    def x_copy(l, h, k):
        return pltpu.make_async_remote_copy(
            src_ref=xs.at[l, h, r],
            dst_ref=xs.at[l, h, r],
            send_sem=xsend.at[l, h, k - 1],
            recv_sem=xrecv.at[l, h, k - 1],
            device_id={"prow": row_peer[k]},
            device_id_type=MESH,
        )

    def p_copy(l, h, k):
        return pltpu.make_async_remote_copy(
            src_ref=part_out.at[l - 1, h, k - 1],
            dst_ref=part_in.at[l - 1, h, k - 1],
            send_sem=psend.at[l - 1, h, k - 1],
            recv_sem=precv.at[l - 1, h, k - 1],
            device_id={"pcol": col_peer[k]},
            device_id_type=MESH,
        )

    def merge(l):
        load(l).wait()
        piece = 32

        def source(s, carry):
            same = {}
            for m in range(nbr):
                for n in range(m + 1, nbr):
                    first = slots[l, s, m]
                    later = slots[l, s, n]
                    same[m, n] = jnp.where(first == later, 1.0, 0.0).astype(F32)
            for i in range(size // piece):
                at = pl.ds(i * piece, piece)
                vals = [raw[l, s * nbr + m, at, :].astype(F32) for m in range(nbr)]
                for m in range(nbr):
                    total = vals[m]
                    for n in range(m + 1, nbr):
                        total = total + same[m, n] * vals[n]
                    merged[l, s * nbr + m, at, :] = total.astype(BF16)
            return carry

        lax.fori_loop(0, rows, source, 0)
        merged[l, per] = jnp.zeros((size, size), BF16)

    def lhs_of(l, h):
        return jnp.concatenate([xs[l, h, s] for s in range(rows)], axis=1)

    def factor(target, owner, l):
        base = ((target * cols + owner) * steps + l) * rows
        return jnp.concatenate([merged[l, table[base + s]] for s in range(rows)], axis=1)

    def deferred(target, first, last):
        def columns(group, carry):
            for i in range(GROUP):
                k = group * GROUP + i
                owner = flip(c, k, cols)
                total = acc[target % 2, k] if first else None
                for l in range(first, last):
                    lhs = jnp.concatenate([lhs_of(l, h) for h in range(CHUNKS)], axis=0)
                    term = dot_nt(lhs, factor(target, owner, l))
                    total = term if total is None else total + term
                acc[target % 2, k] = total
            return carry

        lax.fori_loop(0, cols // GROUP, columns, 0)

    def partials(l, h):
        lhs = lhs_of(l - 1, h)
        at = pl.ds(h * half, half)
        for k in col_order + [0]:
            value = dot_nt(lhs, factor(l, col_peer[k], l - 1))
            if l >= 2:
                value = value + acc[l % 2, k, at, :]
            if k:
                part_out[l - 1, h, k - 1] = value.astype(BF16)
            else:
                own[h] = value
        for k in col_order:
            p_copy(l, h, k).start()

    def solve(l, h):
        at = pl.ds(h * half, half)
        residual = rst[l, at, :]
        if l:
            update = own[h]
            for k in range(1, cols):
                p_copy(l, h, k).wait_recv()
                update = update + part_in[l - 1, h, k - 1].astype(F32)
            residual = residual - update
        solved = dot_nt(residual.astype(BF16), inv[l]).astype(BF16)
        if l < steps:
            xs[l, h, r] = solved
            for k in row_order:
                x_copy(l, h, k).start()
        return solved

    def finish(l, pieces):
        whole = jnp.concatenate([p.astype(F32) for p in pieces], axis=0)
        out[l] = whole.T.astype(BF16)

    rst[0] = rs[0].astype(F32).T
    pl.semaphore_wait(barrier, cols + rows - 2)

    pieces = [solve(0, h) for h in range(CHUNKS)]
    for l in range(1, levels):
        rst[l] = rs[l].astype(F32).T
    merge(0)
    finish(0, pieces)
    for l in range(1, levels):
        for h in range(CHUNKS):
            for k in range(1, rows):
                x_copy(l - 1, h, k).wait_recv()
            partials(l, h)
        if l < steps:
            merge(l)
            deferred(l + 1, l - 1, l)
        pieces = [solve(l, h) for h in range(CHUNKS)]
        finish(l, pieces)
        if l + 2 < levels:
            deferred(l + 2, 0, l)

    for l in range(steps):
        for h in range(CHUNKS):
            for k in range(1, rows):
                x_copy(l, h, k).wait_send()
            for k in range(1, cols):
                p_copy(l + 1, h, k).wait_send()


def body(rows, cols, right_sides, inverses, blocks, targets):
    levels, size, rhs = right_sides.shape[0], right_sides.shape[4], right_sides.shape[5]
    steps = levels - 1
    nbr = targets.shape[-1]
    per = rows * nbr
    half = rhs // CHUNKS
    slots = targets.reshape(steps, rows, nbr) // rows
    place = jnp.arange(per, dtype=jnp.int32).reshape(rows, nbr)
    every = jnp.arange(levels * cols, dtype=jnp.int32)[:, None, None, None]
    table = jnp.min(jnp.where(slots[None] == every, place, per), axis=-1).reshape(-1)
    vmem = pl.BlockSpec(memory_space=pltpu.VMEM)
    smem = pl.BlockSpec(memory_space=pltpu.SMEM)
    solved = pl.pallas_call(
        functools.partial(kernel, (levels, rows, cols, nbr, size, rhs)),
        out_shape=jax.ShapeDtypeStruct((levels, size, rhs), BF16),
        in_specs=[smem, smem, vmem, vmem, pl.BlockSpec(memory_space=pl.ANY)],
        out_specs=vmem,
        scratch_shapes=[
            pltpu.VMEM((steps, per, size, size), BF16),
            pltpu.VMEM((steps, per + 1, size, size), BF16),
            pltpu.VMEM((steps, CHUNKS, rows, half, size), BF16),
            pltpu.VMEM((steps, CHUNKS, cols - 1, half, size), BF16),
            pltpu.VMEM((steps, CHUNKS, cols - 1, half, size), BF16),
            pltpu.VMEM((2, cols, rhs, size), F32),
            pltpu.VMEM((CHUNKS, half, size), F32),
            pltpu.VMEM((levels, rhs, size), F32),
            pltpu.SemaphoreType.DMA((steps,)),
            pltpu.SemaphoreType.DMA((steps, CHUNKS, rows - 1)),
            pltpu.SemaphoreType.DMA((steps, CHUNKS, rows - 1)),
            pltpu.SemaphoreType.DMA((steps, CHUNKS, cols - 1)),
            pltpu.SemaphoreType.DMA((steps, CHUNKS, cols - 1)),
        ],
        compiler_params=pltpu.CompilerParams(
            collective_id=0, has_side_effects=True, vmem_limit_bytes=52 * 1024 * 1024
        ),
    )(
        table,
        slots,
        right_sides.reshape(levels, size, rhs),
        inverses.reshape(levels, size, size),
        blocks.reshape(steps, per, size, size),
    )
    return solved.reshape(right_sides.shape)


def solution(mesh):
    in_specs = (
        P(None, None, "pcol", "prow", None, None),
        P(None, None, "pcol", "prow", None, None),
        P(None, None, "pcol", None, "prow", None, None, None),
        P(None, None, "pcol", None, "prow", None),
    )
    out_specs = P(None, None, "pcol", "prow", None, None)
    inner = functools.partial(body, mesh.shape["prow"], mesh.shape["pcol"])
    return jax.shard_map(inner, mesh=mesh, in_specs=in_specs, out_specs=out_specs, check_vma=False)
```

```python
import functools

import jax
import jax.numpy as jnp
from jax import lax
from jax.experimental import pallas as pl
from jax.experimental.pallas import tpu as pltpu
from jax.sharding import PartitionSpec as P

MESH = pl.DeviceIdType.MESH
CHUNKS = 4
GROUP = 4
F32 = jnp.float32
BF16 = jnp.bfloat16


def dot_nt(a, b):
    return lax.dot_general(a, b, (((1,), (1,)), ((), ())), preferred_element_type=F32)


def flip(a, k, n):
    total = 0
    w = 1
    while w < n:
        total = total + lax.rem(a // w + k // w, 2) * w
        w *= 2
    return total


def kernel(
    dims,
    table,
    slots,
    rs,
    inv,
    blocks,
    out,
    raw,
    merged,
    xs,
    part_in,
    part_out,
    acc,
    own,
    rst,
    load_sem,
    xsend,
    xrecv,
    psend,
    precv,
):
    levels, rows, cols, nbr, size, rhs = dims
    steps = levels - 1
    per = rows * nbr
    half = rhs // CHUNKS
    r = lax.axis_index("prow")
    c = lax.axis_index("pcol")

    col_order = sorted(range(1, cols), key=lambda k: (-bin(k // 2).count("1"), k % 2, k))
    row_order = list(range(rows - 1, 0, -1))
    col_peer = [flip(c, k, cols) for k in range(cols)]
    row_peer = [flip(r, k, rows) for k in range(rows)]

    def load(l):
        return pltpu.make_async_copy(blocks.at[l], raw.at[l], load_sem.at[l])

    for l in range(steps):
        load(l).start()

    barrier = pltpu.get_barrier_semaphore()
    for k in range(1, cols):
        pl.semaphore_signal(
            barrier, inc=1, device_id={"pcol": col_peer[k]}, device_id_type=MESH
        )
    for k in range(1, rows):
        pl.semaphore_signal(
            barrier, inc=1, device_id={"prow": row_peer[k]}, device_id_type=MESH
        )

    def x_copy(l, h, k):
        return pltpu.make_async_remote_copy(
            src_ref=xs.at[l, h, r],
            dst_ref=xs.at[l, h, r],
            send_sem=xsend.at[l],
            recv_sem=xrecv.at[l, h],
            device_id={"prow": row_peer[k]},
            device_id_type=MESH,
        )

    def p_copy(l, h, k):
        return pltpu.make_async_remote_copy(
            src_ref=part_out.at[l - 1, h, k - 1],
            dst_ref=part_in.at[l - 1, h, k - 1],
            send_sem=psend.at[l - 1],
            recv_sem=precv.at[l - 1, h],
            device_id={"pcol": col_peer[k]},
            device_id_type=MESH,
        )

    def waiting(ref, sem):
        pltpu.make_async_copy(ref, ref, sem).wait()

    def merge(l):
        load(l).wait()
        piece = 32

        def source(s, carry):
            same = {}
            for m in range(nbr):
                for n in range(m + 1, nbr):
                    first = slots[l, s, m]
                    later = slots[l, s, n]
                    same[m, n] = jnp.where(first == later, 1.0, 0.0).astype(F32)
            for i in range(size // piece):
                at = pl.ds(i * piece, piece)
                vals = [raw[l, s * nbr + m, at, :].astype(F32) for m in range(nbr)]
                for m in range(nbr):
                    total = vals[m]
                    for n in range(m + 1, nbr):
                        total = total + same[m, n] * vals[n]
                    merged[l, s * nbr + m, at, :] = total.astype(BF16)
            return carry

        lax.fori_loop(0, rows, source, 0)
        merged[l, per] = jnp.zeros((size, size), BF16)

    def lhs_of(l, h):
        return jnp.concatenate([xs[l, h, s] for s in range(rows)], axis=1)

    def factor(target, owner, l):
        base = ((target * cols + owner) * steps + l) * rows
        return jnp.concatenate([merged[l, table[base + s]] for s in range(rows)], axis=1)

    def deferred(target, first, last):
        def columns(group, carry):
            for i in range(GROUP):
                k = group * GROUP + i
                owner = flip(c, k, cols)
                total = acc[target % 2, k] if first else None
                for l in range(first, last):
                    lhs = jnp.concatenate([lhs_of(l, h) for h in range(CHUNKS)], axis=0)
                    term = dot_nt(lhs, factor(target, owner, l))
                    total = term if total is None else total + term
                acc[target % 2, k] = total
            return carry

        lax.fori_loop(0, cols // GROUP, columns, 0)

    def partials(l, h):
        lhs = lhs_of(l - 1, h)
        at = pl.ds(h * half, half)
        for k in col_order + [0]:
            value = dot_nt(lhs, factor(l, col_peer[k], l - 1))
            if l >= 2:
                value = value + acc[l % 2, k, at, :]
            if k:
                part_out[l - 1, h, k - 1] = value.astype(BF16)
            else:
                own[h] = value
        for k in col_order:
            p_copy(l, h, k).start()

    def solve(l, h):
        at = pl.ds(h * half, half)
        residual = rst[l, at, :]
        if l:
            update = own[h]
            waiting(part_in.at[l - 1, h], precv.at[l - 1, h])
            for k in range(1, cols):
                update = update + part_in[l - 1, h, k - 1].astype(F32)
            residual = residual - update
        solved = dot_nt(residual.astype(BF16), inv[l]).astype(BF16)
        if l < steps:
            xs[l, h, r] = solved
            for k in row_order:
                x_copy(l, h, k).start()
        return solved

    def finish(l, pieces):
        whole = jnp.concatenate([p.astype(F32) for p in pieces], axis=0)
        out[l] = whole.T.astype(BF16)

    rst[0] = rs[0].astype(F32).T
    pl.semaphore_wait(barrier, cols + rows - 2)

    pieces = [solve(0, h) for h in range(CHUNKS)]
    for l in range(1, levels):
        rst[l] = rs[l].astype(F32).T
    merge(0)
    finish(0, pieces)
    for l in range(1, levels):
        for h in range(CHUNKS):
            waiting(xs.at[l - 1, h, pl.ds(0, rows - 1)], xrecv.at[l - 1, h])
            partials(l, h)
        if l < steps:
            merge(l)
            deferred(l + 1, l - 1, l)
        pieces = [solve(l, h) for h in range(CHUNKS)]
        finish(l, pieces)
        if l + 2 < levels:
            deferred(l + 2, 0, l)

    for l in range(steps):
        waiting(xs.at[l, :, pl.ds(0, rows - 1)], xsend.at[l])
        waiting(part_out.at[l], psend.at[l])


def body(rows, cols, right_sides, inverses, blocks, targets):
    levels, size, rhs = right_sides.shape[0], right_sides.shape[4], right_sides.shape[5]
    steps = levels - 1
    nbr = targets.shape[-1]
    per = rows * nbr
    half = rhs // CHUNKS
    slots = targets.reshape(steps, rows, nbr) // rows
    place = jnp.arange(per, dtype=jnp.int32).reshape(rows, nbr)
    every = jnp.arange(levels * cols, dtype=jnp.int32)[:, None, None, None]
    table = jnp.min(jnp.where(slots[None] == every, place, per), axis=-1).reshape(-1)
    vmem = pl.BlockSpec(memory_space=pltpu.VMEM)
    smem = pl.BlockSpec(memory_space=pltpu.SMEM)
    solved = pl.pallas_call(
        functools.partial(kernel, (levels, rows, cols, nbr, size, rhs)),
        out_shape=jax.ShapeDtypeStruct((levels, size, rhs), BF16),
        in_specs=[smem, smem, vmem, vmem, pl.BlockSpec(memory_space=pl.ANY)],
        out_specs=vmem,
        scratch_shapes=[
            pltpu.VMEM((steps, per, size, size), BF16),
            pltpu.VMEM((steps, per + 1, size, size), BF16),
            pltpu.VMEM((steps, CHUNKS, rows, half, size), BF16),
            pltpu.VMEM((steps, CHUNKS, cols - 1, half, size), BF16),
            pltpu.VMEM((steps, CHUNKS, cols - 1, half, size), BF16),
            pltpu.VMEM((2, cols, rhs, size), F32),
            pltpu.VMEM((CHUNKS, half, size), F32),
            pltpu.VMEM((levels, rhs, size), F32),
            pltpu.SemaphoreType.DMA((steps,)),
            pltpu.SemaphoreType.DMA((steps,)),
            pltpu.SemaphoreType.DMA((steps, CHUNKS)),
            pltpu.SemaphoreType.DMA((steps,)),
            pltpu.SemaphoreType.DMA((steps, CHUNKS)),
        ],
        compiler_params=pltpu.CompilerParams(
            collective_id=0, has_side_effects=True, vmem_limit_bytes=52 * 1024 * 1024
        ),
    )(
        table,
        slots,
        right_sides.reshape(levels, size, rhs),
        inverses.reshape(levels, size, size),
        blocks.reshape(steps, per, size, size),
    )
    return solved.reshape(right_sides.shape)


def solution(mesh):
    in_specs = (
        P(None, None, "pcol", "prow", None, None),
        P(None, None, "pcol", "prow", None, None),
        P(None, None, "pcol", None, "prow", None, None, None),
        P(None, None, "pcol", None, "prow", None),
    )
    out_specs = P(None, None, "pcol", "prow", None, None)
    inner = functools.partial(body, mesh.shape["prow"], mesh.shape["pcol"])
    return jax.shard_map(inner, mesh=mesh, in_specs=in_specs, out_specs=out_specs, check_vma=False)
```

```python
import functools

import jax
import jax.numpy as jnp
from jax import lax
from jax.experimental import pallas as pl
from jax.experimental.pallas import tpu as pltpu
from jax.sharding import PartitionSpec as P

MESH = pl.DeviceIdType.MESH
CHUNKS = 4
GROUP = 4
F32 = jnp.float32
BF16 = jnp.bfloat16


def dot_nt(a, b):
    return lax.dot_general(a, b, (((1,), (1,)), ((), ())), preferred_element_type=F32)


def flip(a, k, n):
    total = 0
    w = 1
    while w < n:
        total = total + lax.rem(a // w + k // w, 2) * w
        w *= 2
    return total


def kernel(
    dims,
    table,
    slots,
    rs_hbm,
    inv_hbm,
    blocks,
    out,
    raw,
    merged,
    xs,
    part_in,
    part_out,
    acc,
    own,
    rst,
    rs,
    inv,
    in_sem,
    load_sem,
    xsend,
    xrecv,
    psend,
    precv,
):
    levels, rows, cols, nbr, size, rhs = dims
    steps = levels - 1
    per = rows * nbr
    half = rhs // CHUNKS
    r = lax.axis_index("prow")
    c = lax.axis_index("pcol")

    col_order = sorted(range(1, cols), key=lambda k: (-bin(k // 2).count("1"), k % 2, k))
    row_order = list(range(rows - 1, 0, -1))
    col_peer = [flip(c, k, cols) for k in range(cols)]
    row_peer = [flip(r, k, rows) for k in range(rows)]

    def load(l):
        return pltpu.make_async_copy(blocks.at[l], raw.at[l], load_sem.at[l])

    inputs = []
    for at in (pl.ds(0, 1), pl.ds(1, steps)):
        for src, dst in ((rs_hbm, rs), (inv_hbm, inv)):
            sem = in_sem.at[len(inputs)]
            inputs.append(pltpu.make_async_copy(src.at[at], dst.at[at], sem))
    for copy in inputs:
        copy.start()
    for l in range(steps):
        load(l).start()

    barrier = pltpu.get_barrier_semaphore()
    for k in range(1, cols):
        pl.semaphore_signal(
            barrier, inc=1, device_id={"pcol": col_peer[k]}, device_id_type=MESH
        )
    for k in range(1, rows):
        pl.semaphore_signal(
            barrier, inc=1, device_id={"prow": row_peer[k]}, device_id_type=MESH
        )

    def x_copy(l, h, k):
        return pltpu.make_async_remote_copy(
            src_ref=xs.at[l, h, r],
            dst_ref=xs.at[l, h, r],
            send_sem=xsend.at[l],
            recv_sem=xrecv.at[l, h],
            device_id={"prow": row_peer[k]},
            device_id_type=MESH,
        )

    def p_copy(l, h, k):
        return pltpu.make_async_remote_copy(
            src_ref=part_out.at[l - 1, h, k - 1],
            dst_ref=part_in.at[l - 1, h, k - 1],
            send_sem=psend.at[l - 1],
            recv_sem=precv.at[l - 1, h],
            device_id={"pcol": col_peer[k]},
            device_id_type=MESH,
        )

    def waiting(ref, sem):
        pltpu.make_async_copy(ref, ref, sem).wait()

    def merge(l):
        load(l).wait()
        piece = 32

        def source(s, carry):
            same = {}
            for m in range(nbr):
                for n in range(m + 1, nbr):
                    first = slots[l, s, m]
                    later = slots[l, s, n]
                    same[m, n] = jnp.where(first == later, 1.0, 0.0).astype(F32)
            for i in range(size // piece):
                at = pl.ds(i * piece, piece)
                vals = [raw[l, s * nbr + m, at, :].astype(F32) for m in range(nbr)]
                for m in range(nbr):
                    total = vals[m]
                    for n in range(m + 1, nbr):
                        total = total + same[m, n] * vals[n]
                    merged[l, s * nbr + m, at, :] = total.astype(BF16)
            return carry

        lax.fori_loop(0, rows, source, 0)
        merged[l, per] = jnp.zeros((size, size), BF16)

    def lhs_of(l, h):
        return jnp.concatenate([xs[l, h, s] for s in range(rows)], axis=1)

    def factor(target, owner, l):
        at = target * cols + owner
        return jnp.concatenate([merged[l, table[l, s, at]] for s in range(rows)], axis=1)

    def deferred(target, first, last):
        def columns(group, carry):
            for i in range(GROUP):
                k = group * GROUP + i
                owner = flip(c, k, cols)
                total = acc[target % 2, k] if first else None
                for l in range(first, last):
                    lhs = jnp.concatenate([lhs_of(l, h) for h in range(CHUNKS)], axis=0)
                    term = dot_nt(lhs, factor(target, owner, l))
                    total = term if total is None else total + term
                acc[target % 2, k] = total
            return carry

        lax.fori_loop(0, cols // GROUP, columns, 0)

    def partials(l, h):
        lhs = lhs_of(l - 1, h)
        at = pl.ds(h * half, half)
        for k in col_order + [0]:
            value = dot_nt(lhs, factor(l, col_peer[k], l - 1))
            if l >= 2:
                value = value + acc[l % 2, k, at, :]
            if k:
                part_out[l - 1, h, k - 1] = value.astype(BF16)
            else:
                own[h] = value
        for k in col_order:
            p_copy(l, h, k).start()

    def solve(l, h):
        at = pl.ds(h * half, half)
        residual = rst[l, at, :]
        if l:
            update = own[h]
            waiting(part_in.at[l - 1, h], precv.at[l - 1, h])
            for k in range(1, cols):
                update = update + part_in[l - 1, h, k - 1].astype(F32)
            residual = residual - update
        residual = residual.astype(BF16)
        if l == steps:
            return residual
        solved = dot_nt(residual, inv[l]).astype(BF16)
        xs[l, h, r] = solved
        for k in row_order:
            x_copy(l, h, k).start()
        return solved

    def finish(l, pieces):
        whole = jnp.concatenate([p.astype(F32) for p in pieces], axis=0)
        out[l] = whole.T.astype(BF16)

    for copy in inputs[:2]:
        copy.wait()
    rst[0] = rs[0].astype(F32).T
    pl.semaphore_wait(barrier, cols + rows - 2)

    pieces = [solve(0, h) for h in range(CHUNKS)]
    for copy in inputs[2:]:
        copy.wait()
    for l in range(1, levels):
        rst[l] = rs[l].astype(F32).T
    merge(0)
    finish(0, pieces)
    for l in range(1, levels):
        for h in range(CHUNKS):
            waiting(xs.at[l - 1, h, pl.ds(0, rows - 1)], xrecv.at[l - 1, h])
            partials(l, h)
        if l < steps:
            merge(l)
            deferred(l + 1, l - 1, l)
        pieces = [solve(l, h) for h in range(CHUNKS)]
        if l < steps:
            finish(l, pieces)
        else:
            out[l] = dot_nt(inv[l], jnp.concatenate(pieces, axis=0)).astype(BF16)
        if l + 2 < levels:
            deferred(l + 2, 0, l)

    for l in range(steps):
        waiting(xs.at[l, :, pl.ds(0, rows - 1)], xsend.at[l])
        waiting(part_out.at[l], psend.at[l])


def body(rows, cols, right_sides, inverses, blocks, targets):
    levels, size, rhs = right_sides.shape[0], right_sides.shape[4], right_sides.shape[5]
    steps = levels - 1
    nbr = targets.shape[-1]
    per = rows * nbr
    half = rhs // CHUNKS
    slots = targets.reshape(steps, rows, nbr) // rows
    place = jnp.arange(per, dtype=jnp.int32).reshape(rows, nbr)
    every = jnp.arange(levels * cols, dtype=jnp.int32)[None, None, :, None]
    found = slots[:, :, None] == every
    table = jnp.min(jnp.where(found, place[None, :, None], per), axis=-1)
    vmem = pl.BlockSpec(memory_space=pltpu.VMEM)
    smem = pl.BlockSpec(memory_space=pltpu.SMEM)
    solved = pl.pallas_call(
        functools.partial(kernel, (levels, rows, cols, nbr, size, rhs)),
        out_shape=jax.ShapeDtypeStruct((levels, size, rhs), BF16),
        in_specs=[smem, smem] + [pl.BlockSpec(memory_space=pltpu.HBM)] * 3,
        out_specs=vmem,
        scratch_shapes=[
            pltpu.VMEM((steps, per, size, size), BF16),
            pltpu.VMEM((steps, per + 1, size, size), BF16),
            pltpu.VMEM((steps, CHUNKS, rows, half, size), BF16),
            pltpu.VMEM((steps, CHUNKS, cols - 1, half, size), BF16),
            pltpu.VMEM((steps, CHUNKS, cols - 1, half, size), BF16),
            pltpu.VMEM((2, cols, rhs, size), F32),
            pltpu.VMEM((CHUNKS, half, size), F32),
            pltpu.VMEM((levels, rhs, size), F32),
            pltpu.VMEM((levels, size, rhs), BF16),
            pltpu.VMEM((levels, size, size), BF16),
            pltpu.SemaphoreType.DMA((4,)),
            pltpu.SemaphoreType.DMA((steps,)),
            pltpu.SemaphoreType.DMA((steps,)),
            pltpu.SemaphoreType.DMA((steps, CHUNKS)),
            pltpu.SemaphoreType.DMA((steps,)),
            pltpu.SemaphoreType.DMA((steps, CHUNKS)),
        ],
        compiler_params=pltpu.CompilerParams(
            collective_id=0, has_side_effects=True, vmem_limit_bytes=54784 * 1024
        ),
    )(
        table,
        slots,
        right_sides.reshape(levels, size, rhs),
        inverses.reshape(levels, size, size),
        blocks.reshape(steps, per, size, size),
    )
    return solved.reshape(right_sides.shape)


def solution(mesh):
    in_specs = (
        P(None, None, "pcol", "prow", None, None),
        P(None, None, "pcol", "prow", None, None),
        P(None, None, "pcol", None, "prow", None, None, None),
        P(None, None, "pcol", None, "prow", None),
    )
    out_specs = P(None, None, "pcol", "prow", None, None)
    inner = functools.partial(body, mesh.shape["prow"], mesh.shape["pcol"])
    return jax.shard_map(inner, mesh=mesh, in_specs=in_specs, out_specs=out_specs, check_vma=False)
```

```python
import functools

import jax
import jax.numpy as jnp
from jax import lax
from jax.experimental import pallas as pl
from jax.experimental.pallas import tpu as pltpu
from jax.sharding import PartitionSpec as P

MESH = pl.DeviceIdType.MESH
CHUNKS = 4
GROUP = 4
F32 = jnp.float32
BF16 = jnp.bfloat16


def dot_nt(a, b):
    return lax.dot_general(a, b, (((1,), (1,)), ((), ())), preferred_element_type=F32)


def flip(a, k, n):
    total = 0
    w = 1
    while w < n:
        total = total + lax.rem(a // w + k // w, 2) * w
        w *= 2
    return total


def kernel(
    dims,
    numbers,
    rs_hbm,
    inv_hbm,
    blocks,
    out,
    raw,
    merged,
    xs,
    part_in,
    part_out,
    acc,
    own,
    rst,
    rs,
    inv,
    found,
    table,
    slots,
    in_sem,
    load_sem,
    xsend,
    xrecv,
    psend,
    precv,
):
    levels, rows, cols, nbr, size, rhs = dims
    steps = levels - 1
    per = rows * nbr
    half = rhs // CHUNKS
    r = lax.axis_index("prow")
    c = lax.axis_index("pcol")

    col_order = sorted(range(1, cols), key=lambda k: (-bin(k // 2).count("1"), k % 2, k))
    row_order = list(range(rows - 1, 0, -1))
    col_peer = [flip(c, k, cols) for k in range(cols)]
    row_peer = [flip(r, k, rows) for k in range(rows)]

    def load(l):
        return pltpu.make_async_copy(blocks.at[l], raw.at[l], load_sem.at[l])

    inputs = []
    for at in (pl.ds(0, 1), pl.ds(1, steps)):
        for src, dst in ((rs_hbm, rs), (inv_hbm, inv)):
            sem = in_sem.at[len(inputs)]
            inputs.append(pltpu.make_async_copy(src.at[at], dst.at[at], sem))
    for copy in inputs:
        copy.start()
    listing = pltpu.make_async_copy(numbers, slots, in_sem.at[4])
    listing.start()
    for l in range(steps):
        load(l).start()

    barrier = pltpu.get_barrier_semaphore()
    for k in range(1, cols):
        pl.semaphore_signal(
            barrier, inc=1, device_id={"pcol": col_peer[k]}, device_id_type=MESH
        )
    for k in range(1, rows):
        pl.semaphore_signal(
            barrier, inc=1, device_id={"prow": row_peer[k]}, device_id_type=MESH
        )

    def x_copy(l, h, k):
        return pltpu.make_async_remote_copy(
            src_ref=xs.at[l, h, r],
            dst_ref=xs.at[l, h, r],
            send_sem=xsend.at[l],
            recv_sem=xrecv.at[l, h],
            device_id={"prow": row_peer[k]},
            device_id_type=MESH,
        )

    def p_copy(l, h, k):
        return pltpu.make_async_remote_copy(
            src_ref=part_out.at[l - 1, h, k - 1],
            dst_ref=part_in.at[l - 1, h, k - 1],
            send_sem=psend.at[l - 1],
            recv_sem=precv.at[l - 1, h],
            device_id={"pcol": col_peer[k]},
            device_id_type=MESH,
        )

    def waiting(ref, sem):
        pltpu.make_async_copy(ref, ref, sem).wait()

    def index():
        listing.wait()
        wanted = lax.broadcasted_iota(jnp.int32, (1, found.shape[1]), 1) * rows + r

        def line(i, carry):
            base = lax.rem(i, rows) * nbr
            place = jnp.full(wanted.shape, per, jnp.int32)
            for m in reversed(range(nbr)):
                place = jnp.where(wanted == slots[i, 0, m], base + m, place)
            found[pl.ds(i, 1), :] = place
            return carry

        lax.fori_loop(0, steps * rows, line, 0)
        filed = pltpu.make_async_copy(found, table, in_sem.at[5])
        filed.start()
        return filed

    def merge(l):
        load(l).wait()
        piece = 32

        def source(s, carry):
            same = {}
            for m in range(nbr):
                for n in range(m + 1, nbr):
                    first = slots[l * rows + s, 0, m]
                    later = slots[l * rows + s, 0, n]
                    same[m, n] = jnp.where(first == later, 1.0, 0.0).astype(F32)
            for i in range(size // piece):
                at = pl.ds(i * piece, piece)
                vals = [raw[l, s * nbr + m, at, :].astype(F32) for m in range(nbr)]
                for m in range(nbr):
                    total = vals[m]
                    for n in range(m + 1, nbr):
                        total = total + same[m, n] * vals[n]
                    merged[l, s * nbr + m, at, :] = total.astype(BF16)
            return carry

        lax.fori_loop(0, rows, source, 0)
        merged[l, per] = jnp.zeros((size, size), BF16)

    def lhs_of(l, h):
        return jnp.concatenate([xs[l, h, s] for s in range(rows)], axis=1)

    def factor(target, owner, l):
        at = target * cols + owner
        return jnp.concatenate([merged[l, table[l * rows + s, at]] for s in range(rows)], axis=1)

    def deferred(target, first, last):
        def columns(group, carry):
            for i in range(GROUP):
                k = group * GROUP + i
                owner = flip(c, k, cols)
                total = acc[target % 2, k] if first else None
                for l in range(first, last):
                    lhs = jnp.concatenate([lhs_of(l, h) for h in range(CHUNKS)], axis=0)
                    term = dot_nt(lhs, factor(target, owner, l))
                    total = term if total is None else total + term
                acc[target % 2, k] = total
            return carry

        lax.fori_loop(0, cols // GROUP, columns, 0)

    def partials(l, h):
        lhs = lhs_of(l - 1, h)
        at = pl.ds(h * half, half)
        for k in col_order + [0]:
            value = dot_nt(lhs, factor(l, col_peer[k], l - 1))
            if l >= 2:
                value = value + acc[l % 2, k, at, :]
            if k:
                part_out[l - 1, h, k - 1] = value.astype(BF16)
            else:
                own[h] = value
        for k in col_order:
            p_copy(l, h, k).start()

    def send(l, h, value):
        xs[l, h, r] = value
        for k in row_order:
            x_copy(l, h, k).start()

    def solve(l, h):
        at = pl.ds(h * half, half)
        waiting(part_in.at[l - 1, h], precv.at[l - 1, h])
        update = own[h]
        for k in range(1, cols):
            update = update + part_in[l - 1, h, k - 1].astype(F32)
        residual = rst[l, at, :] - update
        residual = residual.astype(BF16)
        if l == steps:
            return residual
        solved = dot_nt(residual, inv[l]).astype(BF16)
        send(l, h, solved)
        return solved

    def finish(l, pieces):
        whole = jnp.concatenate([p.astype(F32) for p in pieces], axis=0)
        out[l] = whole.T.astype(BF16)

    for copy in inputs[:2]:
        copy.wait()
    rst[0] = rs[0].astype(F32).T
    first = dot_nt(rst[0].astype(BF16), inv[0]).astype(BF16)
    pl.semaphore_wait(barrier, cols + rows - 2)

    pieces = [first[h * half : (h + 1) * half] for h in range(CHUNKS)]
    for h in range(CHUNKS):
        send(0, h, pieces[h])
    for copy in inputs[2:]:
        copy.wait()
    for l in range(1, levels):
        rst[l] = rs[l].astype(F32).T
    filed = index()
    merge(0)
    filed.wait()
    finish(0, pieces)
    for l in range(1, levels):
        for h in range(CHUNKS):
            waiting(xs.at[l - 1, h, pl.ds(0, rows - 1)], xrecv.at[l - 1, h])
            partials(l, h)
        if l < steps:
            merge(l)
            deferred(l + 1, l - 1, l)
        pieces = [solve(l, h) for h in range(CHUNKS)]
        if l < steps:
            finish(l, pieces)
        else:
            out[l] = dot_nt(inv[l], jnp.concatenate(pieces, axis=0)).astype(BF16)
        if l + 2 < levels:
            deferred(l + 2, 0, l)

    for l in range(steps):
        waiting(xs.at[l, :, pl.ds(0, rows - 1)], xsend.at[l])
        waiting(part_out.at[l], psend.at[l])


def body(rows, cols, right_sides, inverses, blocks, targets):
    levels, size, rhs = right_sides.shape[0], right_sides.shape[4], right_sides.shape[5]
    steps = levels - 1
    nbr = targets.shape[-1]
    per = rows * nbr
    half = rhs // CHUNKS
    lanes = -(-levels * cols // 128) * 128
    lines = -(-steps * rows // 8) * 8
    vmem = pl.BlockSpec(memory_space=pltpu.VMEM)
    solved = pl.pallas_call(
        functools.partial(kernel, (levels, rows, cols, nbr, size, rhs)),
        out_shape=jax.ShapeDtypeStruct((levels, size, rhs), BF16),
        in_specs=[pl.BlockSpec(memory_space=pltpu.HBM)] * 4,
        out_specs=vmem,
        scratch_shapes=[
            pltpu.VMEM((steps, per, size, size), BF16),
            pltpu.VMEM((steps, per + 1, size, size), BF16),
            pltpu.VMEM((steps, CHUNKS, rows, half, size), BF16),
            pltpu.VMEM((steps, CHUNKS, cols - 1, half, size), BF16),
            pltpu.VMEM((steps, CHUNKS, cols - 1, half, size), BF16),
            pltpu.VMEM((2, cols, rhs, size), F32),
            pltpu.VMEM((CHUNKS, half, size), F32),
            pltpu.VMEM((levels, rhs, size), F32),
            pltpu.VMEM((levels, size, rhs), BF16),
            pltpu.VMEM((levels, size, size), BF16),
            pltpu.VMEM((lines, lanes), jnp.int32),
            pltpu.SMEM((lines, lanes), jnp.int32),
            pltpu.SMEM((steps * rows, 1, nbr), jnp.int32),
            pltpu.SemaphoreType.DMA((6,)),
            pltpu.SemaphoreType.DMA((steps,)),
            pltpu.SemaphoreType.DMA((steps,)),
            pltpu.SemaphoreType.DMA((steps, CHUNKS)),
            pltpu.SemaphoreType.DMA((steps,)),
            pltpu.SemaphoreType.DMA((steps, CHUNKS)),
        ],
        compiler_params=pltpu.CompilerParams(
            collective_id=0, has_side_effects=True, vmem_limit_bytes=54784 * 1024
        ),
    )(
        targets.reshape(steps * rows, 1, nbr),
        right_sides.reshape(levels, size, rhs),
        inverses.reshape(levels, size, size),
        blocks.reshape(steps, per, size, size),
    )
    return solved.reshape(right_sides.shape)


def solution(mesh):
    in_specs = (
        P(None, None, "pcol", "prow", None, None),
        P(None, None, "pcol", "prow", None, None),
        P(None, None, "pcol", None, "prow", None, None, None),
        P(None, None, "pcol", None, "prow", None),
    )
    out_specs = P(None, None, "pcol", "prow", None, None)
    inner = functools.partial(body, mesh.shape["prow"], mesh.shape["pcol"])
    return jax.shard_map(inner, mesh=mesh, in_specs=in_specs, out_specs=out_specs, check_vma=False)
```

```python
import functools

import jax
import jax.numpy as jnp
from jax import lax
from jax.experimental import pallas as pl
from jax.experimental.pallas import tpu as pltpu
from jax.sharding import PartitionSpec as P

MESH = pl.DeviceIdType.MESH
CHUNKS = 4
GROUP = 4
F32 = jnp.float32
BF16 = jnp.bfloat16


def dot_nt(a, b):
    return lax.dot_general(a, b, (((1,), (1,)), ((), ())), preferred_element_type=F32)


def flip(a, k, n):
    total = 0
    w = 1
    while w < n:
        total = total + lax.rem(a // w + k // w, 2) * w
        w *= 2
    return total


def kernel(
    dims,
    numbers,
    rs_hbm,
    inv_hbm,
    blocks,
    out,
    raw,
    merged,
    xs,
    part_in,
    part_out,
    acc,
    own,
    rst,
    rs,
    inv,
    found,
    table,
    slots,
    in_sem,
    load_sem,
    xsend,
    xrecv,
    psend,
    precv,
):
    levels, rows, cols, nbr, size, rhs = dims
    steps = levels - 1
    per = rows * nbr
    half = rhs // CHUNKS
    r = lax.axis_index("prow")
    c = lax.axis_index("pcol")

    col_order = sorted(range(1, cols), key=lambda k: (-bin(k // 2).count("1"), k % 2, k))
    row_order = list(range(rows - 1, 0, -1))
    col_peer = [flip(c, k, cols) for k in range(cols)]
    row_peer = [flip(r, k, rows) for k in range(rows)]

    def load(l):
        return pltpu.make_async_copy(blocks.at[l], raw.at[l], load_sem.at[l])

    inputs = []
    for at in (pl.ds(0, 1), pl.ds(1, steps)):
        for src, dst in ((rs_hbm, rs), (inv_hbm, inv)):
            sem = in_sem.at[len(inputs)]
            inputs.append(pltpu.make_async_copy(src.at[at], dst.at[at], sem))
    for copy in inputs:
        copy.start()
    listing = pltpu.make_async_copy(numbers, slots, in_sem.at[4])
    listing.start()
    for l in range(steps):
        load(l).start()

    barrier = pltpu.get_barrier_semaphore()
    for k in range(1, cols):
        pl.semaphore_signal(
            barrier, inc=1, device_id={"pcol": col_peer[k]}, device_id_type=MESH
        )
    for k in range(1, rows):
        pl.semaphore_signal(
            barrier, inc=1, device_id={"prow": row_peer[k]}, device_id_type=MESH
        )

    def x_copy(l, h, k):
        return pltpu.make_async_remote_copy(
            src_ref=xs.at[l, h, r],
            dst_ref=xs.at[l, h, r],
            send_sem=xsend.at[l],
            recv_sem=xrecv.at[l, h],
            device_id={"prow": row_peer[k]},
            device_id_type=MESH,
        )

    def p_copy(l, h, k):
        return pltpu.make_async_remote_copy(
            src_ref=part_out.at[l - 1, h, k - 1],
            dst_ref=part_in.at[l - 1, h, k - 1],
            send_sem=psend.at[l - 1],
            recv_sem=precv.at[l - 1, h],
            device_id={"pcol": col_peer[k]},
            device_id_type=MESH,
        )

    def waiting(ref, sem):
        pltpu.make_async_copy(ref, ref, sem).wait()

    def index():
        listing.wait()
        wanted = lax.broadcasted_iota(jnp.int32, (1, found.shape[1]), 1) * rows + r

        def line(i, carry):
            base = lax.rem(i, rows) * nbr
            place = jnp.full(wanted.shape, per, jnp.int32)
            for m in reversed(range(nbr)):
                place = jnp.where(wanted == slots[i, 0, m], base + m, place)
            found[pl.ds(i, 1), :] = place
            return carry

        lax.fori_loop(0, steps * rows, line, 0)
        filed = pltpu.make_async_copy(found, table, in_sem.at[5])
        filed.start()
        return filed

    def merge(l):
        load(l).wait()
        piece = 32

        def source(s, carry):
            same = {}
            for m in range(nbr):
                for n in range(m + 1, nbr):
                    first = slots[l * rows + s, 0, m]
                    later = slots[l * rows + s, 0, n]
                    same[m, n] = jnp.where(first == later, 1.0, 0.0).astype(F32)
            for i in range(size // piece):
                at = pl.ds(i * piece, piece)
                vals = [raw[l, s * nbr + m, at, :].astype(F32) for m in range(nbr)]
                for m in range(nbr):
                    total = vals[m]
                    for n in range(m + 1, nbr):
                        total = total + same[m, n] * vals[n]
                    merged[l, s * nbr + m, at, :] = total.astype(BF16)
            return carry

        lax.fori_loop(0, rows, source, 0)
        merged[l, per] = jnp.zeros((size, size), BF16)

    def lhs_of(l, h):
        return jnp.concatenate([xs[l, h, s] for s in range(rows)], axis=1)

    def factor(target, owner, l):
        at = target * cols + owner
        return jnp.concatenate([merged[l, table[l * rows + s, at]] for s in range(rows)], axis=1)

    def deferred(target, first, last):
        def columns(group, carry):
            for i in range(GROUP):
                k = group * GROUP + i
                owner = flip(c, k, cols)
                total = acc[target % 2, k] if first else None
                for l in range(first, last):
                    lhs = jnp.concatenate([lhs_of(l, h) for h in range(CHUNKS)], axis=0)
                    term = dot_nt(lhs, factor(target, owner, l))
                    total = term if total is None else total + term
                acc[target % 2, k] = total
            return carry

        lax.fori_loop(0, cols // GROUP, columns, 0)

    def partials(l, h):
        lhs = lhs_of(l - 1, h)
        at = pl.ds(h * half, half)
        for k in col_order + [0]:
            value = dot_nt(lhs, factor(l, col_peer[k], l - 1))
            if l >= 2:
                value = value + acc[l % 2, k, at, :]
            if k:
                part_out[l - 1, h, k - 1] = value.astype(BF16)
            else:
                own[h] = value
        for k in col_order:
            p_copy(l, h, k).start()

    def send(l, h, value):
        xs[l, h, r] = value
        for k in row_order:
            x_copy(l, h, k).start()

    def solve(l, h):
        at = pl.ds(h * half, half)
        waiting(part_in.at[l - 1, h], precv.at[l - 1, h])
        update = own[h]
        for k in range(1, cols):
            update = update + part_in[l - 1, h, k - 1].astype(F32)
        residual = rst[l, at, :] - update
        residual = residual.astype(BF16)
        if l == steps:
            return residual
        solved = dot_nt(residual, inv[l]).astype(BF16)
        send(l, h, solved)
        return solved

    def finish(l, pieces):
        whole = jnp.concatenate([p.astype(F32) for p in pieces], axis=0)
        out[l] = whole.T.astype(BF16)

    for copy in inputs[:2]:
        copy.wait()
    rst[0] = rs[0].astype(F32).T
    first = dot_nt(rst[0].astype(BF16), inv[0]).astype(BF16)
    pl.semaphore_wait(barrier, cols + rows - 2)

    pieces = [first[h * half : (h + 1) * half] for h in range(CHUNKS)]
    for h in range(CHUNKS):
        send(0, h, pieces[h])
    for copy in inputs[2:]:
        copy.wait()
    for l in range(1, levels):
        rst[l] = rs[l].astype(F32).T
    filed = index()
    merge(0)
    filed.wait()
    finish(0, pieces)
    for l in range(1, levels):
        for h in range(CHUNKS):
            waiting(xs.at[l - 1, h, pl.ds(0, rows - 1)], xrecv.at[l - 1, h])
            partials(l, h)
        if l < steps:
            merge(l)
            deferred(l + 1, l - 1, l)
        pieces = [solve(l, h) for h in range(CHUNKS)]
        if l < steps:
            finish(l, pieces)
        else:
            out[l] = dot_nt(inv[l], jnp.concatenate(pieces, axis=0)).astype(BF16)
        if l + 2 < levels:
            deferred(l + 2, 0, l)
        waiting(xs.at[l - 1, :, pl.ds(0, rows - 1)], xsend.at[l - 1])
        if l < steps:
            waiting(part_out.at[l - 1], psend.at[l - 1])

    waiting(part_out.at[steps - 1], psend.at[steps - 1])


def body(rows, cols, right_sides, inverses, blocks, targets):
    levels, size, rhs = right_sides.shape[0], right_sides.shape[4], right_sides.shape[5]
    steps = levels - 1
    nbr = targets.shape[-1]
    per = rows * nbr
    half = rhs // CHUNKS
    lanes = -(-levels * cols // 128) * 128
    lines = -(-steps * rows // 8) * 8
    vmem = pl.BlockSpec(memory_space=pltpu.VMEM)
    solved = pl.pallas_call(
        functools.partial(kernel, (levels, rows, cols, nbr, size, rhs)),
        out_shape=jax.ShapeDtypeStruct((levels, size, rhs), BF16),
        in_specs=[pl.BlockSpec(memory_space=pltpu.HBM)] * 4,
        out_specs=vmem,
        scratch_shapes=[
            pltpu.VMEM((steps, per, size, size), BF16),
            pltpu.VMEM((steps, per + 1, size, size), BF16),
            pltpu.VMEM((steps, CHUNKS, rows, half, size), BF16),
            pltpu.VMEM((steps, CHUNKS, cols - 1, half, size), BF16),
            pltpu.VMEM((steps, CHUNKS, cols - 1, half, size), BF16),
            pltpu.VMEM((2, cols, rhs, size), F32),
            pltpu.VMEM((CHUNKS, half, size), F32),
            pltpu.VMEM((levels, rhs, size), F32),
            pltpu.VMEM((levels, size, rhs), BF16),
            pltpu.VMEM((levels, size, size), BF16),
            pltpu.VMEM((lines, lanes), jnp.int32),
            pltpu.SMEM((lines, lanes), jnp.int32),
            pltpu.SMEM((steps * rows, 1, nbr), jnp.int32),
            pltpu.SemaphoreType.DMA((6,)),
            pltpu.SemaphoreType.DMA((steps,)),
            pltpu.SemaphoreType.DMA((steps,)),
            pltpu.SemaphoreType.DMA((steps, CHUNKS)),
            pltpu.SemaphoreType.DMA((steps,)),
            pltpu.SemaphoreType.DMA((steps, CHUNKS)),
        ],
        compiler_params=pltpu.CompilerParams(
            collective_id=0, has_side_effects=True, vmem_limit_bytes=54784 * 1024
        ),
    )(
        targets.reshape(steps * rows, 1, nbr),
        right_sides.reshape(levels, size, rhs),
        inverses.reshape(levels, size, size),
        blocks.reshape(steps, per, size, size),
    )
    return solved.reshape(right_sides.shape)


def solution(mesh):
    in_specs = (
        P(None, None, "pcol", "prow", None, None),
        P(None, None, "pcol", "prow", None, None),
        P(None, None, "pcol", None, "prow", None, None, None),
        P(None, None, "pcol", None, "prow", None),
    )
    out_specs = P(None, None, "pcol", "prow", None, None)
    inner = functools.partial(body, mesh.shape["prow"], mesh.shape["pcol"])
    return jax.shard_map(inner, mesh=mesh, in_specs=in_specs, out_specs=out_specs, check_vma=False)
```

```python
import functools

import jax
import jax.numpy as jnp
from jax import lax
from jax.experimental import pallas as pl
from jax.experimental.pallas import tpu as pltpu
from jax.sharding import PartitionSpec as P

MESH = pl.DeviceIdType.MESH
CHUNKS = 4
GROUP = 8
F32 = jnp.float32
BF16 = jnp.bfloat16


def dot_nt(a, b):
    return lax.dot_general(a, b, (((1,), (1,)), ((), ())), preferred_element_type=F32)


def flip(a, k, n):
    total = 0
    w = 1
    while w < n:
        total = total + lax.rem(a // w + k // w, 2) * w
        w *= 2
    return total


def kernel(
    dims,
    numbers,
    rs_hbm,
    inv_hbm,
    blocks,
    out,
    raw,
    merged,
    xs,
    part_in,
    part_out,
    acc,
    own,
    rst,
    rs,
    inv,
    found,
    table,
    slots,
    in_sem,
    load_sem,
    xsend,
    xrecv,
    psend,
    precv,
):
    levels, rows, cols, nbr, size, rhs = dims
    steps = levels - 1
    per = rows * nbr
    half = rhs // CHUNKS
    r = lax.axis_index("prow")
    c = lax.axis_index("pcol")

    col_order = sorted(range(1, cols), key=lambda k: (-bin(k // 2).count("1"), k % 2, k))
    row_order = list(range(rows - 1, 0, -1))
    col_peer = [flip(c, k, cols) for k in range(cols)]
    row_peer = [flip(r, k, rows) for k in range(rows)]

    def load(l):
        return pltpu.make_async_copy(blocks.at[l], raw.at[l], load_sem.at[l])

    inputs = []
    for at in (pl.ds(0, 1), pl.ds(1, steps)):
        for src, dst in ((rs_hbm, rs), (inv_hbm, inv)):
            sem = in_sem.at[len(inputs)]
            inputs.append(pltpu.make_async_copy(src.at[at], dst.at[at], sem))
    for copy in inputs:
        copy.start()
    listing = pltpu.make_async_copy(numbers, slots, in_sem.at[4])
    listing.start()
    for l in range(steps):
        load(l).start()

    barrier = pltpu.get_barrier_semaphore()
    for k in range(1, cols):
        pl.semaphore_signal(
            barrier, inc=1, device_id={"pcol": col_peer[k]}, device_id_type=MESH
        )
    for k in range(1, rows):
        pl.semaphore_signal(
            barrier, inc=1, device_id={"prow": row_peer[k]}, device_id_type=MESH
        )

    def x_copy(l, h, k):
        return pltpu.make_async_remote_copy(
            src_ref=xs.at[l, h, r],
            dst_ref=xs.at[l, h, r],
            send_sem=xsend.at[l],
            recv_sem=xrecv.at[l, h],
            device_id={"prow": row_peer[k]},
            device_id_type=MESH,
        )

    def p_copy(l, h, k):
        return pltpu.make_async_remote_copy(
            src_ref=part_out.at[l - 1, h, k - 1],
            dst_ref=part_in.at[l - 1, h, k - 1],
            send_sem=psend.at[l - 1],
            recv_sem=precv.at[l - 1, h],
            device_id={"pcol": col_peer[k]},
            device_id_type=MESH,
        )

    def waiting(ref, sem):
        pltpu.make_async_copy(ref, ref, sem).wait()

    def index():
        listing.wait()
        wanted = lax.broadcasted_iota(jnp.int32, (1, found.shape[1]), 1) * rows + r

        def line(i, carry):
            base = lax.rem(i, rows) * nbr
            place = jnp.full(wanted.shape, per, jnp.int32)
            for m in reversed(range(nbr)):
                place = jnp.where(wanted == slots[i, 0, m], base + m, place)
            found[pl.ds(i, 1), :] = place
            return carry

        lax.fori_loop(0, steps * rows, line, 0)
        filed = pltpu.make_async_copy(found, table, in_sem.at[5])
        filed.start()
        return filed

    def merge(l):
        load(l).wait()
        piece = 32

        def source(s, carry):
            same = {}
            for m in range(nbr):
                for n in range(m + 1, nbr):
                    first = slots[l * rows + s, 0, m]
                    later = slots[l * rows + s, 0, n]
                    same[m, n] = jnp.where(first == later, 1.0, 0.0).astype(F32)
            for i in range(size // piece):
                at = pl.ds(i * piece, piece)
                vals = [raw[l, s * nbr + m, at, :].astype(F32) for m in range(nbr)]
                for m in range(nbr):
                    total = vals[m]
                    for n in range(m + 1, nbr):
                        total = total + same[m, n] * vals[n]
                    merged[l, s * nbr + m, at, :] = total.astype(BF16)
            return carry

        lax.fori_loop(0, rows, source, 0)
        merged[l, per] = jnp.zeros((size, size), BF16)

    def lhs_of(l, h):
        return jnp.concatenate([xs[l, h, s] for s in range(rows)], axis=1)

    def factor(target, owner, l):
        at = target * cols + owner
        return jnp.concatenate([merged[l, table[l * rows + s, at]] for s in range(rows)], axis=1)

    def deferred(target, first, last):
        def columns(group, carry):
            for i in range(GROUP):
                k = group * GROUP + i
                owner = flip(c, k, cols)
                total = acc[target % 2, k] if first else None
                for l in range(first, last):
                    lhs = jnp.concatenate([lhs_of(l, h) for h in range(CHUNKS)], axis=0)
                    term = dot_nt(lhs, factor(target, owner, l))
                    total = term if total is None else total + term
                acc[target % 2, k] = total
            return carry

        lax.fori_loop(0, cols // GROUP, columns, 0)

    def partials(l, h):
        lhs = lhs_of(l - 1, h)
        at = pl.ds(h * half, half)
        ks = col_order + [0]
        for batch in (ks[: cols // 2], ks[cols // 2 :]):
            for k in batch:
                value = dot_nt(lhs, factor(l, col_peer[k], l - 1))
                if l >= 2:
                    value = value + acc[l % 2, k, at, :]
                if k:
                    part_out[l - 1, h, k - 1] = value.astype(BF16)
                else:
                    own[h] = value
            for k in batch:
                if k:
                    p_copy(l, h, k).start()

    def send(l, h, value):
        xs[l, h, r] = value
        for k in row_order:
            x_copy(l, h, k).start()

    def solve(l, h):
        at = pl.ds(h * half, half)
        waiting(part_in.at[l - 1, h], precv.at[l - 1, h])
        update = own[h]
        for k in range(1, cols):
            update = update + part_in[l - 1, h, k - 1].astype(F32)
        residual = rst[l, at, :] - update
        residual = residual.astype(BF16)
        if l == steps:
            return residual
        solved = dot_nt(residual, inv[l]).astype(BF16)
        send(l, h, solved)
        return solved

    def finish(l, pieces):
        whole = jnp.concatenate([p.astype(F32) for p in pieces], axis=0)
        out[l] = whole.T.astype(BF16)

    for copy in inputs[:2]:
        copy.wait()
    rst[0] = rs[0].astype(F32).T
    first = dot_nt(rst[0].astype(BF16), inv[0]).astype(BF16)
    pl.semaphore_wait(barrier, cols + rows - 2)

    pieces = [first[h * half : (h + 1) * half] for h in range(CHUNKS)]
    for h in range(CHUNKS):
        send(0, h, pieces[h])
    for copy in inputs[2:]:
        copy.wait()
    for l in range(1, levels):
        rst[l] = rs[l].astype(F32).T
    filed = index()
    merge(0)
    filed.wait()
    finish(0, pieces)
    for l in range(1, levels):
        for h in range(CHUNKS):
            waiting(xs.at[l - 1, h, pl.ds(0, rows - 1)], xrecv.at[l - 1, h])
            partials(l, h)
        if l < steps:
            merge(l)
            deferred(l + 1, l - 1, l)
        pieces = [solve(l, h) for h in range(CHUNKS)]
        if l < steps:
            finish(l, pieces)
        else:
            out[l] = dot_nt(inv[l], jnp.concatenate(pieces, axis=0)).astype(BF16)
        if l + 2 < levels:
            deferred(l + 2, 0, l)
        waiting(xs.at[l - 1, :, pl.ds(0, rows - 1)], xsend.at[l - 1])
        if l < steps:
            waiting(part_out.at[l - 1], psend.at[l - 1])

    waiting(part_out.at[steps - 1], psend.at[steps - 1])


def body(rows, cols, right_sides, inverses, blocks, targets):
    levels, size, rhs = right_sides.shape[0], right_sides.shape[4], right_sides.shape[5]
    steps = levels - 1
    nbr = targets.shape[-1]
    per = rows * nbr
    half = rhs // CHUNKS
    lanes = -(-levels * cols // 128) * 128
    lines = -(-steps * rows // 8) * 8
    vmem = pl.BlockSpec(memory_space=pltpu.VMEM)
    solved = pl.pallas_call(
        functools.partial(kernel, (levels, rows, cols, nbr, size, rhs)),
        out_shape=jax.ShapeDtypeStruct((levels, size, rhs), BF16),
        in_specs=[pl.BlockSpec(memory_space=pltpu.HBM)] * 4,
        out_specs=vmem,
        scratch_shapes=[
            pltpu.VMEM((steps, per, size, size), BF16),
            pltpu.VMEM((steps, per + 1, size, size), BF16),
            pltpu.VMEM((steps, CHUNKS, rows, half, size), BF16),
            pltpu.VMEM((steps, CHUNKS, cols - 1, half, size), BF16),
            pltpu.VMEM((steps, CHUNKS, cols - 1, half, size), BF16),
            pltpu.VMEM((2, cols, rhs, size), F32),
            pltpu.VMEM((CHUNKS, half, size), F32),
            pltpu.VMEM((levels, rhs, size), F32),
            pltpu.VMEM((levels, size, rhs), BF16),
            pltpu.VMEM((levels, size, size), BF16),
            pltpu.VMEM((lines, lanes), jnp.int32),
            pltpu.SMEM((lines, lanes), jnp.int32),
            pltpu.SMEM((steps * rows, 1, nbr), jnp.int32),
            pltpu.SemaphoreType.DMA((6,)),
            pltpu.SemaphoreType.DMA((steps,)),
            pltpu.SemaphoreType.DMA((steps,)),
            pltpu.SemaphoreType.DMA((steps, CHUNKS)),
            pltpu.SemaphoreType.DMA((steps,)),
            pltpu.SemaphoreType.DMA((steps, CHUNKS)),
        ],
        compiler_params=pltpu.CompilerParams(
            collective_id=0, has_side_effects=True, vmem_limit_bytes=54784 * 1024
        ),
    )(
        targets.reshape(steps * rows, 1, nbr),
        right_sides.reshape(levels, size, rhs),
        inverses.reshape(levels, size, size),
        blocks.reshape(steps, per, size, size),
    )
    return solved.reshape(right_sides.shape)


def solution(mesh):
    in_specs = (
        P(None, None, "pcol", "prow", None, None),
        P(None, None, "pcol", "prow", None, None),
        P(None, None, "pcol", None, "prow", None, None, None),
        P(None, None, "pcol", None, "prow", None),
    )
    out_specs = P(None, None, "pcol", "prow", None, None)
    inner = functools.partial(body, mesh.shape["prow"], mesh.shape["pcol"])
    return jax.shard_map(inner, mesh=mesh, in_specs=in_specs, out_specs=out_specs, check_vma=False)
```
